256 devices in a mesh: gx: 16 (over x, y_lo, core), gy: 16 (over y_hi, z).
Axes of the slice: x: 4, y: 4 (y_hi: 2, y_lo: 2; y = y_hi * 2 + y_lo), z: 8, core: 2. Of those that a mesh axis runs over, the one named last changes fastest.
Arguments:
- tokens: bfloat16 [512, 8192], P('gy', 'gx'), may hold values from -6 to 6
- gate_first: bfloat16 [8192, 28672], P('gx', 'gy'), may hold values from -0.0625 to 0.0625
- up_first: bfloat16 [8192, 28672], P('gx', 'gy'), may hold values from -0.0625 to 0.0625
- down_first: bfloat16 [28672, 8192], P('gy', 'gx'), may hold values from -0.0625 to 0.0625
- gate_second: bfloat16 [8192, 28672], P('gx', 'gy'), may hold values from -0.0625 to 0.0625
- up_second: bfloat16 [8192, 28672], P('gx', 'gy'), may hold values from -0.0625 to 0.0625
- down_second: bfloat16 [28672, 8192], P('gy', 'gx'), may hold values from -0.0625 to 0.0625
Outputs:
- second_out: float32 [512, 8192], P('gy', 'gx')
The draws below stay inside these ranges and needn't reach their ends.
All inputs are finite; a program needn't handle non-finite values.
Results may differ from the reference program's by a relative error of at most 0.0085.
Values may be sent and summed in bfloat16 or wider, within the bound.
A program may use at most 64 MiB of HBM per device.

```python
import jax
import jax.numpy as jnp

D = 8192
FF = 28672
BATCH = 512


def level_of(key, dims, split, least, largest):
    loudness, own = 1.0, jax.random.fold_in(key, 6)
    for position, shards_of in split:
        steps = jnp.exp(jax.random.uniform(jax.random.fold_in(own, position), (shards_of,), jnp.float32, least / len(split), largest / len(split)))
        loudness = loudness * jnp.repeat(steps, dims[position] // shards_of).reshape([-1 if axis == position else 1 for axis in range(len(dims))])
    return loudness


def centred(own_key, dims, width, limit, cuts=(), dtype=jnp.bfloat16):
    gain = level_of(own_key, dims, cuts, -0.22, 0.18) if cuts else 1.0
    array = jax.random.normal(own_key, dims, jnp.float32) * width * gain
    return jnp.minimum(jnp.maximum(array, -limit), limit).astype(dtype)


def setup_inputs(seed: int = 0) -> dict:
    seeds = jax.random.split(jax.random.key(seed), 8)
    return {
        "tokens": centred(seeds[0], (BATCH, D), 1.0, 6.0, ((0, 16), (1, 16))),
        "gate_first": centred(seeds[1], (D, FF), D ** -0.5, 0.0625, ((0, 16), (1, 16))),
        "up_first": centred(seeds[2], (D, FF), D ** -0.5, 0.0625, ((0, 16), (1, 16))),
        "down_first": centred(seeds[3], (FF, D), (FF // 4) ** -0.5, 0.0625, ((0, 16), (1, 16))),
        "gate_second": centred(seeds[4], (D, FF), D ** -0.5, 0.0625, ((0, 16), (1, 16))),
        "up_second": centred(seeds[5], (D, FF), D ** -0.5, 0.0625, ((0, 16), (1, 16))),
        "down_second": centred(seeds[6], (FF, D), (FF // 4) ** -0.5, 0.0625, ((0, 16), (1, 16))),
    }


def feed_forward(inputs, gate_weight, up_weight, down_weight):
    gate_sum = jnp.dot(inputs, gate_weight, preferred_element_type=jnp.float32)
    up_sum = jnp.dot(inputs, up_weight, preferred_element_type=jnp.float32)
    hidden = (jax.nn.silu(gate_sum) * up_sum).astype(jnp.bfloat16)
    return jnp.dot(hidden, down_weight, preferred_element_type=jnp.float32)


def reference(tokens, gate_first, up_first, down_first, gate_second, up_second, down_second):
    first_out = feed_forward(tokens, gate_first, up_first, down_first).astype(jnp.bfloat16)
    return feed_forward(first_out, gate_second, up_second, down_second)
```

```python
import functools

import jax
import jax.numpy as jnp
from jax import lax
from jax.experimental import pallas as pl
from jax.experimental.pallas import tpu as pltpu
from jax.sharding import PartitionSpec as P

HALVES = 2
ROWS = 16
WIDTH = 512
HIDDEN = 1792
CHUNKS = ((0, 512), (512, 640), (1152, 640))
NC = len(CHUNKS)
OFFSETS = tuple((dx, dy) for dx in range(4) for dy in range(2) if dx + dy > 0)
BF16 = jnp.bfloat16
F32 = jnp.float32


def wait_bytes(ref, sem):
    pltpu.make_async_copy(ref, ref, sem).wait()


def kernel(
    tokens, g0, u0, d0, g1, u1, d1, out,
    wg, wu, wd, tok, part, crecv, rsend, rrecv, hid, acc, zsend, zrecv, ysum, yrecv,
    w_s, c_s, r_s, a_s, f_s, z_s, y_s, t_s, i_s,
):
    gx, gy = lax.axis_index("gx"), lax.axis_index("gy")
    c, chip = lax.rem(gx, 2), gx // 2
    yl, x = lax.rem(chip, 2), chip // 2
    z, yh = lax.rem(gy, 8), gy // 8

    def remote(src, dst, sems, index, device):
        pltpu.make_async_remote_copy(
            src_ref=src, dst_ref=dst, send_sem=sems.at[(0, *index)], recv_sem=sems.at[(1, *index)],
            device_id=device, device_id_type=pl.DeviceIdType.MESH,
        ).start()

    other_core = (chip * 2 + 1 - c, gy)
    other_half = (gx, (1 - yh) * 8 + z)

    def chip_at(dx, dy):
        return lax.rem(x + dx, 4) * 2 + lax.rem(yl + dy, 2)

    def z_at(dz):
        return lax.rem(z + dz, 8)

    for n, (src, dst) in enumerate(
        ((g0, wg.at[0]), (u0, wu.at[0]), (d0, wd.at[0]), (g1, wg.at[1]), (u1, wu.at[1]), (d1, wd.at[1]))
    ):
        pltpu.make_async_copy(src, dst, w_s.at[n]).start()

    def wait_weight(n):
        ref = (wg, wu, wd)[n % 3].at[n // 3]
        wait_bytes(ref, w_s.at[n])

    def first_send(h):
        tok[0, h, yh, z] = tokens[pl.ds(ROWS * h, ROWS), :]
        mine = tok.at[0, h, yh, z]
        remote(mine, mine, i_s, (0, h), other_half)
        for dz in range(1, 8):
            remote(mine, mine, i_s, (1, h), (gx, yh * 8 + z_at(dz)))

    def first_forward(h):
        theirs = tok.at[0, h, 1 - yh, z]
        wait_bytes(theirs, i_s.at[1, 0, h])
        for dz in range(1, 8):
            remote(theirs, theirs, i_s, (2, h), (gx, yh * 8 + z_at(dz)))

    def first_wait(h):
        for n in (1, 2):
            wait_bytes(tok.at[0, h, 0, pl.ds(0, 7)], i_s.at[1, n, h])

    def gate_up(l, h, i):
        at, w = CHUNKS[i]
        value = tok[l, h].reshape(2 * 8 * ROWS, WIDTH)
        for n, weight in enumerate((wg, wu)):
            done = jnp.dot(value, weight[l, :, at : at + w], preferred_element_type=F32)
            part[h, :, :, :, 2 * at + n * w : 2 * at + n * w + w] = done.reshape(2, 8, ROWS, w)
        cols = pl.ds(2 * at, 2 * w)
        remote(part.at[h, 1 - c, :, :, cols], crecv.at[h, :, :, cols], c_s, (l, h, i), other_core)

    def scatter(l, h, i):
        at, w = CHUNKS[i]
        cols = pl.ds(2 * at, 2 * w)
        wait_bytes(crecv.at[h, :, :, cols], c_s.at[1, l, h, i])
        crecv[h, :, :, cols] = part[h, c, :, :, cols] + crecv[h, :, :, cols]
        rsend[l, h, :, :, cols] = crecv[h, :, :, cols].astype(BF16)
        for t, offset in enumerate(OFFSETS):
            to = chip_at(*offset)
            remote(rsend.at[l, h, to, :, cols], rrecv.at[l, h, t, :, cols], r_s, (l, h, i), (to * 2 + c, gy))

    def activate(l, h, i):
        at, w = CHUNKS[i]
        cols = pl.ds(2 * at, 2 * w)
        wait_bytes(rrecv.at[l, h, :, :, cols], r_s.at[1, l, h, i])
        total = crecv[h, chip, :, cols]
        for t in range(7):
            total = total + rrecv[l, h, t, :, cols].astype(F32)
        gate, up = total[:, :w], total[:, w:]
        hcols = pl.ds(at, w)
        hid[l, h, c, chip, :, hcols] = (gate / (1.0 + jnp.exp(-gate)) * up).astype(BF16)
        mine = hid.at[l, h, c, chip, :, hcols]
        for offset in OFFSETS:
            remote(mine, mine, a_s, (l, h, i), (chip_at(*offset) * 2 + c, gy))

    def forward(l, h, i):
        at, w = CHUNKS[i]
        hcols = pl.ds(at, w)
        wait_bytes(hid.at[l, h, 0, pl.ds(0, 7), :, hcols], a_s.at[1, l, h, i])
        rows = hid.at[l, h, c, :, :, hcols]
        remote(rows, rows, f_s, (l, h, i), other_core)

    def down(l, h, i):
        at, w = CHUNKS[i]
        hcols = pl.ds(at, w)
        wait_bytes(hid.at[l, h, 0, :, :, hcols], f_s.at[1, l, h, i])
        value = hid[l, h, :, :, :, hcols].reshape(2 * 8 * ROWS, w)
        done = jnp.dot(value, wd[l, at : at + w, :], preferred_element_type=F32).reshape(2, 8, ROWS, WIDTH)
        if i > 0:
            done = acc[h] + done
        acc[h] = done
        if i == NC - 1:
            zsend[l, h] = done.astype(BF16)
            for dz in range(1, 8):
                to = z_at(dz)
                remote(zsend.at[l, h, :, to], zrecv.at[l, h, dz - 1], z_s, (l, h), (gx, yh * 8 + to))

    def reduce_z(l, h):
        wait_bytes(zrecv.at[l, h], z_s.at[1, l, h])
        total = acc[h, :, z]
        for n in range(7):
            total = total + zrecv[l, h, n].astype(F32)
        ysum[l, h] = total
        if l == 0:
            remote(ysum.at[l, h], yrecv.at[l, h], y_s, (l, h), other_half)
        else:
            remote(ysum.at[l, h, 1 - yh], yrecv.at[l, h, 0], y_s, (l, h), other_half)

    def gather_z(h):
        wait_bytes(yrecv.at[0, h], y_s.at[1, 0, h])
        tok[1, h, :, z] = (ysum[0, h] + yrecv[0, h]).astype(BF16)
        mine = tok.at[1, h, :, z]
        for dz in range(1, 8):
            remote(mine, mine, t_s, (h,), (gx, yh * 8 + z_at(dz)))

    def gather_wait(h):
        wait_bytes(tok.at[1, h, :, pl.ds(0, 7)], t_s.at[1, h])

    def finish(h):
        wait_bytes(yrecv.at[1, h, 0], y_s.at[1, 1, h])
        out[pl.ds(ROWS * h, ROWS), :] = ysum[1, h, yh] + yrecv[1, h, 0]

    def send_core(l, h):
        for i in range(NC):
            at, w = CHUNKS[i]
            wait_bytes(crecv.at[h, :, :, pl.ds(2 * at, 2 * w)], c_s.at[0, l, h, i])

    first_send(0)
    first_send(1)
    first_forward(0)
    first_forward(1)
    for l in range(2):
        for h in range(HALVES):
            if l == 0:
                first_wait(h)
            else:
                gather_wait(h)
                send_core(0, h)
            if h == 0:
                wait_weight(3 * l)
                wait_weight(3 * l + 1)
            for i in range(NC):
                gate_up(l, h, i)
            for i in range(NC):
                scatter(l, h, i)
            if l == 1 and h == 0:
                reduce_z(0, 1)
                gather_z(1)
        wait_weight(3 * l + 2)
        for h in range(HALVES):
            activate(l, h, 0)
            for i in range(1, NC):
                activate(l, h, i)
                forward(l, h, i - 1)
            for i in range(NC):
                if i == 0:
                    forward(l, h, NC - 1)
                down(l, h, i)
        reduce_z(l, 0)
        if l == 0:
            gather_z(0)
    finish(0)
    reduce_z(1, 1)
    finish(1)

    for h in range(HALVES):
        block = tok.at[0, h, 0, 0]
        wait_bytes(block, i_s.at[0, 0, h])
        for n in (1, 2):
            wait_bytes(tok.at[0, h, 0, pl.ds(0, 7)], i_s.at[0, n, h])
        wait_bytes(tok.at[1, h, :, pl.ds(0, 7)], t_s.at[0, h])
        send_core(1, h)
        wait_bytes(yrecv.at[0, h], y_s.at[0, 0, h])
        wait_bytes(yrecv.at[1, h, 0], y_s.at[0, 1, h])
        for l in range(2):
            wait_bytes(zrecv.at[l, h], z_s.at[0, l, h])
            for i in range(NC):
                at, w = CHUNKS[i]
                hcols = pl.ds(at, w)
                wait_bytes(rrecv.at[l, h, :, :, pl.ds(2 * at, 2 * w)], r_s.at[0, l, h, i])
                wait_bytes(hid.at[l, h, 0, pl.ds(0, 7), :, hcols], a_s.at[0, l, h, i])
                wait_bytes(hid.at[l, h, 0, :, :, hcols], f_s.at[0, l, h, i])


def shards(*arrays):
    vmem = pl.BlockSpec(memory_space=pltpu.VMEM)
    anywhere = pl.BlockSpec(memory_space=pl.ANY)
    L, H = 2, HALVES
    sem = pltpu.SemaphoreType.DMA
    return pl.pallas_call(
        kernel,
        out_shape=jax.ShapeDtypeStruct((HALVES * ROWS, WIDTH), F32),
        in_specs=[vmem] + [anywhere] * 6,
        out_specs=vmem,
        scratch_shapes=[
            pltpu.VMEM((L, WIDTH, HIDDEN), BF16),
            pltpu.VMEM((L, WIDTH, HIDDEN), BF16),
            pltpu.VMEM((L, HIDDEN, WIDTH), BF16),
            pltpu.VMEM((L, H, 2, 8, ROWS, WIDTH), BF16),
            pltpu.VMEM((H, 2, 8, ROWS, 2 * HIDDEN), F32),
            pltpu.VMEM((H, 8, ROWS, 2 * HIDDEN), F32),
            pltpu.VMEM((L, H, 8, ROWS, 2 * HIDDEN), BF16),
            pltpu.VMEM((L, H, 7, ROWS, 2 * HIDDEN), BF16),
            pltpu.VMEM((L, H, 2, 8, ROWS, HIDDEN), BF16),
            pltpu.VMEM((H, 2, 8, ROWS, WIDTH), F32),
            pltpu.VMEM((L, H, 2, 8, ROWS, WIDTH), BF16),
            pltpu.VMEM((L, H, 7, 2, ROWS, WIDTH), BF16),
            pltpu.VMEM((L, H, 2, ROWS, WIDTH), F32),
            pltpu.VMEM((L, H, 2, ROWS, WIDTH), F32),
            sem((6,)),
            sem((2, L, H, NC)),
            sem((2, L, H, NC)),
            sem((2, L, H, NC)),
            sem((2, L, H, NC)),
            sem((2, L, H)),
            sem((2, L, H)),
            sem((2, H)),
            sem((2, 3, H)),
        ],
        compiler_params=pltpu.CompilerParams(has_side_effects=True, vmem_limit_bytes=56 * 2**20),
        cost_estimate=pl.CostEstimate(flops=6 * 2 * 512 * 512 * 1792, bytes_accessed=6 * 512 * 1792 * 2, transcendentals=0),
    )(*arrays)


def solution(mesh):
    in_specs = (
        P("gy", "gx"),
        P("gx", "gy"),
        P("gx", "gy"),
        P("gy", "gx"),
        P("gx", "gy"),
        P("gx", "gy"),
        P("gy", "gx"),
    )
    return jax.shard_map(shards, mesh=mesh, in_specs=in_specs, out_specs=P("gy", "gx"), check_vma=False)
```

```python
import functools

import jax
import jax.numpy as jnp
from jax import lax
from jax.experimental import pallas as pl
from jax.experimental.pallas import tpu as pltpu
from jax.sharding import PartitionSpec as P

HALVES = 2
ROWS = 16
WIDTH = 512
HIDDEN = 1792
CHUNKS = ((0, 512), (512, 640), (1152, 640))
NC = len(CHUNKS)
OFFSETS = tuple((dx, dy) for dx in range(4) for dy in range(2) if dx + dy > 0)
BF16 = jnp.bfloat16
F32 = jnp.float32


def wait_bytes(ref, sem):
    pltpu.make_async_copy(ref, ref, sem).wait()


def kernel(
    tokens, g0, u0, d0, g1, u1, d1, out,
    wg, wu, wd, tok, part, crecv, rsend, rrecv, hid, acc, zsend, zrecv, ysum, yrecv,
    w_s, c_s, r_s, a_s, f_s, z_s, y_s, t_s, i_s,
):
    gx, gy = lax.axis_index("gx"), lax.axis_index("gy")
    c, chip = lax.rem(gx, 2), gx // 2
    yl, x = lax.rem(chip, 2), chip // 2
    z, yh = lax.rem(gy, 8), gy // 8

    def remote(src, dst, sems, index, device):
        pltpu.make_async_remote_copy(
            src_ref=src, dst_ref=dst, send_sem=sems.at[(0, *index)], recv_sem=sems.at[(1, *index)],
            device_id=device, device_id_type=pl.DeviceIdType.MESH,
        ).start()

    other_core = (chip * 2 + 1 - c, gy)
    other_half = (gx, (1 - yh) * 8 + z)

    def chip_at(dx, dy):
        return lax.rem(x + dx, 4) * 2 + lax.rem(yl + dy, 2)

    def z_at(dz):
        return lax.rem(z + dz, 8)

    partners = [other_core, other_half]
    partners += [(chip_at(*offset) * 2 + c, gy) for offset in OFFSETS]
    partners += [(gx, yh * 8 + z_at(dz)) for dz in range(1, 8)]
    barrier = pltpu.get_barrier_semaphore()
    for device in partners:
        pl.semaphore_signal(barrier, inc=1, device_id=device, device_id_type=pl.DeviceIdType.MESH)

    for n, (src, dst) in enumerate(
        ((g0, wg.at[0]), (u0, wu.at[0]), (d0, wd.at[0]), (g1, wg.at[1]), (u1, wu.at[1]), (d1, wd.at[1]))
    ):
        pltpu.make_async_copy(src, dst, w_s.at[n]).start()

    def wait_weight(n):
        ref = (wg, wu, wd)[n % 3].at[n // 3]
        wait_bytes(ref, w_s.at[n])

    pl.semaphore_wait(barrier, len(partners))

    def first_send(h):
        tok[0, h, yh, z] = tokens[pl.ds(ROWS * h, ROWS), :]
        mine = tok.at[0, h, yh, z]
        remote(mine, mine, i_s, (0, h), other_half)
        for dz in range(1, 8):
            remote(mine, mine, i_s, (1, h), (gx, yh * 8 + z_at(dz)))

    def first_forward(h):
        theirs = tok.at[0, h, 1 - yh, z]
        wait_bytes(theirs, i_s.at[1, 0, h])
        for dz in range(1, 8):
            remote(theirs, theirs, i_s, (2, h), (gx, yh * 8 + z_at(dz)))

    def first_wait(h):
        for n in (1, 2):
            wait_bytes(tok.at[0, h, 0, pl.ds(0, 7)], i_s.at[1, n, h])

    def gate_up(l, h, i):
        at, w = CHUNKS[i]
        value = tok[l, h].reshape(2 * 8 * ROWS, WIDTH)
        for n, weight in enumerate((wg, wu)):
            done = jnp.dot(value, weight[l, :, at : at + w], preferred_element_type=F32)
            part[h, :, :, :, 2 * at + n * w : 2 * at + n * w + w] = done.reshape(2, 8, ROWS, w)
        cols = pl.ds(2 * at, 2 * w)
        remote(part.at[h, 1 - c, :, :, cols], crecv.at[h, :, :, cols], c_s, (l, h, i), other_core)

    def scatter(l, h, i):
        at, w = CHUNKS[i]
        cols = pl.ds(2 * at, 2 * w)
        wait_bytes(crecv.at[h, :, :, cols], c_s.at[1, l, h, i])
        crecv[h, :, :, cols] = part[h, c, :, :, cols] + crecv[h, :, :, cols]
        rsend[l, h, :, :, cols] = crecv[h, :, :, cols].astype(BF16)
        for t, offset in enumerate(OFFSETS):
            to = chip_at(*offset)
            remote(rsend.at[l, h, to, :, cols], rrecv.at[l, h, t, :, cols], r_s, (l, h, i), (to * 2 + c, gy))

    def activate(l, h, i):
        at, w = CHUNKS[i]
        cols = pl.ds(2 * at, 2 * w)
        wait_bytes(rrecv.at[l, h, :, :, cols], r_s.at[1, l, h, i])
        total = crecv[h, chip, :, cols]
        for t in range(7):
            total = total + rrecv[l, h, t, :, cols].astype(F32)
        gate, up = total[:, :w], total[:, w:]
        hcols = pl.ds(at, w)
        hid[l, h, c, chip, :, hcols] = (gate / (1.0 + jnp.exp(-gate)) * up).astype(BF16)
        mine = hid.at[l, h, c, chip, :, hcols]
        for offset in OFFSETS:
            remote(mine, mine, a_s, (l, h, i), (chip_at(*offset) * 2 + c, gy))

    def forward(l, h, i):
        at, w = CHUNKS[i]
        hcols = pl.ds(at, w)
        wait_bytes(hid.at[l, h, 0, pl.ds(0, 7), :, hcols], a_s.at[1, l, h, i])
        rows = hid.at[l, h, c, :, :, hcols]
        remote(rows, rows, f_s, (l, h, i), other_core)

    def down(l, h, i):
        at, w = CHUNKS[i]
        hcols = pl.ds(at, w)
        wait_bytes(hid.at[l, h, 0, :, :, hcols], f_s.at[1, l, h, i])
        value = hid[l, h, :, :, :, hcols].reshape(2 * 8 * ROWS, w)
        done = jnp.dot(value, wd[l, at : at + w, :], preferred_element_type=F32).reshape(2, 8, ROWS, WIDTH)
        if i > 0:
            done = acc[h] + done
        acc[h] = done
        if i == NC - 1:
            zsend[l, h] = done.astype(BF16)
            for dz in range(1, 8):
                to = z_at(dz)
                remote(zsend.at[l, h, :, to], zrecv.at[l, h, dz - 1], z_s, (l, h), (gx, yh * 8 + to))

    def reduce_z(l, h):
        wait_bytes(zrecv.at[l, h], z_s.at[1, l, h])
        total = acc[h, :, z]
        for n in range(7):
            total = total + zrecv[l, h, n].astype(F32)
        ysum[l, h] = total
        if l == 0:
            remote(ysum.at[l, h], yrecv.at[l, h], y_s, (l, h), other_half)
        else:
            remote(ysum.at[l, h, 1 - yh], yrecv.at[l, h, 0], y_s, (l, h), other_half)

    def gather_z(h):
        wait_bytes(yrecv.at[0, h], y_s.at[1, 0, h])
        tok[1, h, :, z] = (ysum[0, h] + yrecv[0, h]).astype(BF16)
        mine = tok.at[1, h, :, z]
        for dz in range(1, 8):
            remote(mine, mine, t_s, (h,), (gx, yh * 8 + z_at(dz)))

    def gather_wait(h):
        wait_bytes(tok.at[1, h, :, pl.ds(0, 7)], t_s.at[1, h])

    def finish(h):
        wait_bytes(yrecv.at[1, h, 0], y_s.at[1, 1, h])
        out[pl.ds(ROWS * h, ROWS), :] = ysum[1, h, yh] + yrecv[1, h, 0]

    def send_core(l, h):
        for i in range(NC):
            at, w = CHUNKS[i]
            wait_bytes(crecv.at[h, :, :, pl.ds(2 * at, 2 * w)], c_s.at[0, l, h, i])

    for h in range(HALVES):
        first_send(h)
        first_forward(h)
    for l in range(2):
        for h in range(HALVES):
            if l == 0:
                first_wait(h)
            else:
                gather_wait(h)
                send_core(0, h)
            if h == 0:
                wait_weight(3 * l)
                wait_weight(3 * l + 1)
            for i in range(NC):
                gate_up(l, h, i)
            for i in range(NC):
                scatter(l, h, i)
        wait_weight(3 * l + 2)
        for h in range(HALVES):
            for i in range(NC):
                activate(l, h, i)
        for h in range(HALVES):
            for i in range(NC):
                forward(l, h, i)
            for i in range(NC):
                down(l, h, i)
        for h in range(HALVES):
            reduce_z(l, h)
            if l == 0:
                gather_z(h)
    finish(0)
    finish(1)

    for h in range(HALVES):
        block = tok.at[0, h, 0, 0]
        wait_bytes(block, i_s.at[0, 0, h])
        for n in (1, 2):
            wait_bytes(tok.at[0, h, 0, pl.ds(0, 7)], i_s.at[0, n, h])
        wait_bytes(tok.at[1, h, :, pl.ds(0, 7)], t_s.at[0, h])
        send_core(1, h)
        wait_bytes(yrecv.at[0, h], y_s.at[0, 0, h])
        wait_bytes(yrecv.at[1, h, 0], y_s.at[0, 1, h])
        for l in range(2):
            wait_bytes(zrecv.at[l, h], z_s.at[0, l, h])
            for i in range(NC):
                at, w = CHUNKS[i]
                hcols = pl.ds(at, w)
                wait_bytes(rrecv.at[l, h, :, :, pl.ds(2 * at, 2 * w)], r_s.at[0, l, h, i])
                wait_bytes(hid.at[l, h, 0, pl.ds(0, 7), :, hcols], a_s.at[0, l, h, i])
                wait_bytes(hid.at[l, h, 0, :, :, hcols], f_s.at[0, l, h, i])


def shards(*arrays):
    vmem = pl.BlockSpec(memory_space=pltpu.VMEM)
    anywhere = pl.BlockSpec(memory_space=pl.ANY)
    L, H = 2, HALVES
    sem = pltpu.SemaphoreType.DMA
    return pl.pallas_call(
        kernel,
        out_shape=jax.ShapeDtypeStruct((HALVES * ROWS, WIDTH), F32),
        in_specs=[vmem] + [anywhere] * 6,
        out_specs=vmem,
        scratch_shapes=[
            pltpu.VMEM((L, WIDTH, HIDDEN), BF16),
            pltpu.VMEM((L, WIDTH, HIDDEN), BF16),
            pltpu.VMEM((L, HIDDEN, WIDTH), BF16),
            pltpu.VMEM((L, H, 2, 8, ROWS, WIDTH), BF16),
            pltpu.VMEM((H, 2, 8, ROWS, 2 * HIDDEN), F32),
            pltpu.VMEM((H, 8, ROWS, 2 * HIDDEN), F32),
            pltpu.VMEM((L, H, 8, ROWS, 2 * HIDDEN), BF16),
            pltpu.VMEM((L, H, 7, ROWS, 2 * HIDDEN), BF16),
            pltpu.VMEM((L, H, 2, 8, ROWS, HIDDEN), BF16),
            pltpu.VMEM((H, 2, 8, ROWS, WIDTH), F32),
            pltpu.VMEM((L, H, 2, 8, ROWS, WIDTH), BF16),
            pltpu.VMEM((L, H, 7, 2, ROWS, WIDTH), BF16),
            pltpu.VMEM((L, H, 2, ROWS, WIDTH), F32),
            pltpu.VMEM((L, H, 2, ROWS, WIDTH), F32),
            sem((6,)),
            sem((2, L, H, NC)),
            sem((2, L, H, NC)),
            sem((2, L, H, NC)),
            sem((2, L, H, NC)),
            sem((2, L, H)),
            sem((2, L, H)),
            sem((2, H)),
            sem((2, 3, H)),
        ],
        compiler_params=pltpu.CompilerParams(collective_id=0, has_side_effects=True, vmem_limit_bytes=56 * 2**20),
        cost_estimate=pl.CostEstimate(flops=6 * 2 * 512 * 512 * 1792, bytes_accessed=6 * 512 * 1792 * 2, transcendentals=0),
    )(*arrays)


def solution(mesh):
    in_specs = (
        P("gy", "gx"),
        P("gx", "gy"),
        P("gx", "gy"),
        P("gy", "gx"),
        P("gx", "gy"),
        P("gx", "gy"),
        P("gy", "gx"),
    )
    return jax.shard_map(shards, mesh=mesh, in_specs=in_specs, out_specs=P("gy", "gx"), check_vma=False)
```

```python
import jax
import jax.numpy as jnp
from jax import lax
from jax.experimental import pallas as pl
from jax.experimental.pallas import tpu as pltpu
from jax.sharding import PartitionSpec as P

PARTS = tuple((h, q) for h in range(2) for q in range(2))
ROWS = 16
WIDTH = 512
HALF = 896
OFFSETS = tuple((dx, dy) for dx in range(4) for dy in range(2) if dx + dy > 0)
BF16 = jnp.bfloat16
F32 = jnp.float32
ORDER = (
    ("gate_up", 0, 0), ("gate_up", 0, 1), ("scatter0", 0, 0), ("scatter1", 0, 0),
    ("gate_up", 0, 2), ("scatter0", 0, 1), ("gate_up", 0, 3), ("scatter1", 0, 1),
    ("scatter0", 0, 2), ("middle0", 0, 0), ("middle1", 0, 0), ("scatter1", 0, 2),
    ("scatter0", 0, 3), ("middle0", 0, 1), ("scatter1", 0, 3), ("middle1", 0, 1),
    ("middle0", 0, 2), ("activate", 0, 0), ("middle1", 0, 2), ("middle0", 0, 3),
    ("activate", 0, 1), ("middle1", 0, 3), ("activate", 0, 2), ("forward", 0, 0),
    ("down", 0, 0), ("forward", 0, 1), ("activate", 0, 3), ("down", 0, 1),
    ("forward", 0, 2), ("down", 0, 2), ("reduce_z", 0, 0), ("forward", 0, 3),
    ("down", 0, 3), ("reduce_z", 0, 1), ("gather_z", 0, 0), ("reduce_z", 0, 2),
    ("gather_z", 0, 1), ("reduce_z", 0, 3), ("gather_z", 0, 2), ("gate_up", 1, 0),
    ("gather_z", 0, 3), ("scatter0", 1, 0), ("gate_up", 1, 1), ("scatter1", 1, 0),
    ("gate_up", 1, 2), ("scatter1", 1, 1), ("scatter0", 1, 1), ("middle0", 1, 0),
    ("gate_up", 1, 3), ("middle1", 1, 0), ("scatter1", 1, 2), ("scatter0", 1, 2),
    ("scatter0", 1, 3), ("middle1", 1, 1), ("scatter1", 1, 3), ("middle0", 1, 1),
    ("activate", 1, 0), ("middle1", 1, 2), ("middle0", 1, 2), ("middle1", 1, 3),
    ("middle0", 1, 3), ("activate", 1, 1), ("forward", 1, 0), ("activate", 1, 2),
    ("down", 1, 0), ("activate", 1, 3), ("forward", 1, 1), ("down", 1, 1),
    ("forward", 1, 2), ("down", 1, 2), ("reduce_z", 1, 0), ("forward", 1, 3),
    ("down", 1, 3), ("gather_z", 1, 0), ("reduce_z", 1, 1), ("reduce_z", 1, 2),
    ("gather_z", 1, 1), ("reduce_z", 1, 3), ("gather_z", 1, 2), ("gather_z", 1, 3),
)


def wait_bytes(ref, sem):
    pltpu.make_async_copy(ref, ref, sem).wait()


def kernel(
    tokens, g0, u0, d0, g1, u1, d1, out,
    wgu, wd, tok, pown, pother, crecv, xsend, xrecv, ysend, yback, msend, mrecv, nsend, nrecv, mown, hid, acc, zsend, zrecv, ysum, yrecv,
    w_s, c_s, r_s, m_s, a_s, f_s, z_s, y_s, t_s, i_s,
):
    gx, gy = lax.axis_index("gx"), lax.axis_index("gy")
    c, chip = lax.rem(gx, 2), gx // 2
    yl, x = lax.rem(chip, 2), chip // 2
    z, yh = lax.rem(gy, 8), gy // 8

    def remote(src, dst, sems, index, device):
        pltpu.make_async_remote_copy(
            src_ref=src, dst_ref=dst, send_sem=sems.at[(0, *index)], recv_sem=sems.at[(1, *index)],
            device_id=device, device_id_type=pl.DeviceIdType.MESH,
        ).start()

    other_core = (chip * 2 + 1 - c, gy)
    other_half = (gx, (1 - yh) * 8 + z)
    other_y = ((x * 2 + 1 - yl) * 2 + c, gy)

    def chip_at(dx, dy):
        return lax.rem(x + dx, 4) * 2 + lax.rem(yl + dy, 2)

    def z_at(dz):
        return lax.rem(z + dz, 8)

    partners = [other_core, other_half]
    partners += [(chip_at(*offset) * 2 + c, gy) for offset in OFFSETS]
    partners += [(gx, yh * 8 + z_at(dz)) for dz in range(1, 8)]
    barrier = pltpu.get_barrier_semaphore()
    for device in partners:
        pl.semaphore_signal(barrier, inc=1, device_id=device, device_id_type=pl.DeviceIdType.MESH)

    weights = ((g0, u0, d0), (g1, u1, d1))
    halves = [pl.ds(k * HALF, HALF) for k in range(2)]

    def weight_copies(l):
        gate, up, down = weights[l]
        for k in range(2):
            for n, weight in enumerate((gate, up)):
                pltpu.make_async_copy(weight.at[:, halves[k]], wgu.at[l, k, n], w_s.at[l, 0, k, n]).start()
        for k in range(2):
            pltpu.make_async_copy(down.at[halves[k], :], wd.at[l, k], w_s.at[l, 1, k, 0]).start()

    weight_copies(0)
    weight_copies(1)
    for h in range(2):
        tok[0, h, yh, z] = tokens[pl.ds(ROWS * h, ROWS), :]
    pl.semaphore_wait(barrier, len(partners))

    def first_send(h):
        mine = tok.at[0, h, yh, z]
        remote(mine, mine, i_s, (0, h), other_half)

    def first_own(h):
        mine = tok.at[0, h, yh, z]
        for dz in range(1, 8):
            remote(mine, mine, i_s, (1, h), (gx, yh * 8 + z_at(dz)))

    def first_forward(h):
        theirs = tok.at[0, h, 1 - yh, z]
        wait_bytes(theirs, i_s.at[1, 0, h])
        for dz in range(1, 8):
            remote(theirs, theirs, i_s, (2, h), (gx, yh * 8 + z_at(dz)))

    def gate_up(l, s):
        h, q = PARTS[s]
        if l == 0:
            if q == 0:
                for n in (1, 2):
                    wait_bytes(tok.at[0, h, 0, pl.ds(0, 7)], i_s.at[1, n, h])
        else:
            wait_bytes(tok.at[1, h, q, pl.ds(0, 7)], t_s.at[1, s])
            for n in range(2):
                wait_bytes(crecv.at[s, n], c_s.at[0, 0, s, n])
        if s == 0:
            for k in range(2):
                for n in range(2):
                    wait_bytes(wgu.at[l, k, n], w_s.at[l, 0, k, n])
        value = tok[l, h, q].reshape(8 * ROWS, WIDTH)
        for n in range(2):
            done = jnp.dot(value, wgu[l, 1 - c, n], preferred_element_type=F32)
            pother[s, n] = done.reshape(4, 2, ROWS, HALF)
            remote(pother.at[s, n], crecv.at[s, n], c_s, (l, s, n), other_core)
        for n in range(2):
            done = jnp.dot(value, wgu[l, c, n], preferred_element_type=F32)
            pown[s, n] = done.reshape(4, 2, ROWS, HALF)

    def scatter(l, s, n):
        wait_bytes(crecv.at[s, n], c_s.at[1, l, s, n])
        if n == 0:
            xsend[l, s] = (pown[s, 0] + crecv[s, 0]).astype(BF16)
            for dx in range(1, 4):
                to = lax.rem(x + dx, 4)
                remote(xsend.at[l, s, to], xrecv.at[l, s, dx - 1], r_s, (l, s, 0), ((to * 2 + yl) * 2 + c, gy))
        else:
            ysend[l, s] = (pown[s, 1, :, 1 - yl] + crecv[s, 1, :, 1 - yl]).astype(BF16)
            remote(ysend.at[l, s], yback.at[l, s], r_s, (l, s, 1), other_y)

    def middle(l, s, n):
        if n == 0:
            wait_bytes(xrecv.at[l, s], r_s.at[1, l, s, 0])
            for side in (1 - yl, yl):
                total = pown[s, 0, x, side] + crecv[s, 0, x, side]
                for t in range(3):
                    total = total + xrecv[l, s, t, side].astype(F32)
                if side is yl:
                    mown[s, 0] = total
                else:
                    msend[l, s] = total.astype(BF16)
                    remote(msend.at[l, s], mrecv.at[l, s], m_s, (l, s, 0), other_y)
        else:
            wait_bytes(yback.at[l, s], r_s.at[1, l, s, 1])
            nsend[l, s] = (pown[s, 1, :, yl] + crecv[s, 1, :, yl] + yback[l, s].astype(F32)).astype(BF16)
            for dx in range(1, 4):
                to = lax.rem(x + dx, 4)
                remote(nsend.at[l, s, to], nrecv.at[l, s, dx - 1], m_s, (l, s, 1), ((to * 2 + yl) * 2 + c, gy))
            mown[s, 1] = pown[s, 1, x, yl] + crecv[s, 1, x, yl] + yback[l, s, x].astype(F32)

    def activate(l, s):
        wait_bytes(mrecv.at[l, s], m_s.at[1, l, s, 0])
        gate = mown[s, 0] + mrecv[l, s].astype(F32)
        wait_bytes(nrecv.at[l, s], m_s.at[1, l, s, 1])
        up = mown[s, 1]
        for t in range(3):
            up = up + nrecv[l, s, t].astype(F32)
        hid[l, s, c, chip] = (gate / (1.0 + jnp.exp(-gate)) * up).astype(BF16)
        mine = hid.at[l, s, c, chip]
        for offset in OFFSETS:
            remote(mine, mine, a_s, (l, s), (chip_at(*offset) * 2 + c, gy))

    def half_down(l, s, k):
        value = hid[l, s, k].reshape(8 * ROWS, HALF)
        return jnp.dot(value, wd[l, k], preferred_element_type=F32).reshape(8, ROWS, WIDTH)

    def forward(l, s):
        wait_bytes(hid.at[l, s, 0, pl.ds(0, 7)], a_s.at[1, l, s])
        rows = hid.at[l, s, c]
        remote(rows, rows, f_s, (l, s), other_core)
        if s == 0:
            for k in range(2):
                wait_bytes(wd.at[l, k], w_s.at[l, 1, k, 0])
        acc[s] = half_down(l, s, c)

    def down(l, s):
        wait_bytes(hid.at[l, s, 0], f_s.at[1, l, s])
        done = acc[s] + half_down(l, s, 1 - c)
        acc[s] = done
        zsend[l, s] = done.astype(BF16)
        for dz in range(1, 8):
            to = z_at(dz)
            remote(zsend.at[l, s, to], zrecv.at[l, s, dz - 1], z_s, (l, s), (gx, yh * 8 + to))

    def reduce_z(l, s):
        wait_bytes(zrecv.at[l, s], z_s.at[1, l, s])
        total = acc[s, z]
        for n in range(7):
            total = total + zrecv[l, s, n].astype(F32)
        ysum[l, s] = total
        remote(ysum.at[l, s], yrecv.at[l, s], y_s, (l, s), other_half)

    def gather_z(l, s):
        h, q = PARTS[s]
        wait_bytes(yrecv.at[l, s], y_s.at[1, l, s])
        total = ysum[l, s] + yrecv[l, s]
        if l == 0:
            tok[1, h, q, z] = total.astype(BF16)
            mine = tok.at[1, h, q, z]
            for dz in range(1, 8):
                remote(mine, mine, t_s, (s,), (gx, yh * 8 + z_at(dz)))
        else:

            @pl.when(yh == q)
            def _():
                out[pl.ds(ROWS * h, ROWS), :] = total

    steps = {
        "gate_up": gate_up,
        "scatter0": lambda l, s: scatter(l, s, 0),
        "scatter1": lambda l, s: scatter(l, s, 1),
        "middle0": lambda l, s: middle(l, s, 0),
        "middle1": lambda l, s: middle(l, s, 1),
        "activate": activate,
        "forward": forward,
        "down": down,
        "reduce_z": reduce_z,
        "gather_z": gather_z,
    }
    first_send(0)
    first_own(0)
    first_send(1)
    first_forward(0)
    first_own(1)
    first_forward(1)
    for name, l, s in ORDER:
        steps[name](l, s)

    for h in range(2):
        wait_bytes(tok.at[0, h, 0, 0], i_s.at[0, 0, h])
        for n in (1, 2):
            wait_bytes(tok.at[0, h, 0, pl.ds(0, 7)], i_s.at[0, n, h])
    for s in range(4):
        h, q = PARTS[s]
        wait_bytes(tok.at[1, h, q, pl.ds(0, 7)], t_s.at[0, s])
        for l in range(2):
            for n in range(2):
                if l == 1:
                    wait_bytes(crecv.at[s, n], c_s.at[0, l, s, n])
                wait_bytes((xrecv, yback)[n].at[l, s], r_s.at[0, l, s, n])
                wait_bytes((mrecv, nrecv)[n].at[l, s], m_s.at[0, l, s, n])
            wait_bytes(hid.at[l, s, 0, pl.ds(0, 7)], a_s.at[0, l, s])
            wait_bytes(hid.at[l, s, 0], f_s.at[0, l, s])
            wait_bytes(zrecv.at[l, s], z_s.at[0, l, s])
            wait_bytes(yrecv.at[l, s], y_s.at[0, l, s])


def shards(*arrays):
    vmem = pl.BlockSpec(memory_space=pltpu.VMEM)
    anywhere = pl.BlockSpec(memory_space=pl.ANY)
    L, S = 2, len(PARTS)
    sem = pltpu.SemaphoreType.DMA
    return pl.pallas_call(
        kernel,
        out_shape=jax.ShapeDtypeStruct((2 * ROWS, WIDTH), F32),
        in_specs=[vmem] + [anywhere] * 6,
        out_specs=vmem,
        scratch_shapes=[
            pltpu.VMEM((L, 2, 2, WIDTH, HALF), BF16),
            pltpu.VMEM((L, 2, HALF, WIDTH), BF16),
            pltpu.VMEM((L, 2, 2, 8, ROWS, WIDTH), BF16),
            pltpu.VMEM((S, 2, 4, 2, ROWS, HALF), F32),
            pltpu.VMEM((S, 2, 4, 2, ROWS, HALF), F32),
            pltpu.VMEM((S, 2, 4, 2, ROWS, HALF), F32),
            pltpu.VMEM((L, S, 4, 2, ROWS, HALF), BF16),
            pltpu.VMEM((L, S, 3, 2, ROWS, HALF), BF16),
            pltpu.VMEM((L, S, 4, ROWS, HALF), BF16),
            pltpu.VMEM((L, S, 4, ROWS, HALF), BF16),
            pltpu.VMEM((L, S, ROWS, HALF), BF16),
            pltpu.VMEM((L, S, ROWS, HALF), BF16),
            pltpu.VMEM((L, S, 4, ROWS, HALF), BF16),
            pltpu.VMEM((L, S, 3, ROWS, HALF), BF16),
            pltpu.VMEM((S, 2, ROWS, HALF), F32),
            pltpu.VMEM((L, S, 2, 8, ROWS, HALF), BF16),
            pltpu.VMEM((S, 8, ROWS, WIDTH), F32),
            pltpu.VMEM((L, S, 8, ROWS, WIDTH), BF16),
            pltpu.VMEM((L, S, 7, ROWS, WIDTH), BF16),
            pltpu.VMEM((L, S, ROWS, WIDTH), F32),
            pltpu.VMEM((L, S, ROWS, WIDTH), F32),
            sem((L, 2, 2, 2)),
            sem((2, L, S, 2)),
            sem((2, L, S, 2)),
            sem((2, L, S, 2)),
            sem((2, L, S)),
            sem((2, L, S)),
            sem((2, L, S)),
            sem((2, L, S)),
            sem((2, S)),
            sem((2, 3, 2)),
        ],
        compiler_params=pltpu.CompilerParams(collective_id=0, has_side_effects=True, vmem_limit_bytes=56 * 2**20),
        cost_estimate=pl.CostEstimate(flops=6 * 2 * 512 * 512 * 1792, bytes_accessed=6 * 512 * 1792 * 2, transcendentals=0),
    )(*arrays)


def solution(mesh):
    weights = (P("gx", "gy"), P("gx", "gy"), P("gy", "gx"))
    in_specs = (P("gy", "gx"), *weights, *weights)
    return jax.shard_map(shards, mesh=mesh, in_specs=in_specs, out_specs=P("gy", "gx"), check_vma=False)
```

```python
import jax
import jax.numpy as jnp
from jax import lax
from jax.experimental import pallas as pl
from jax.experimental.pallas import tpu as pltpu
from jax.sharding import PartitionSpec as P

PARTS = tuple((h, q) for h in range(2) for q in range(2))
ROWS = 16
WIDTH = 512
HALF = 896
OFFSETS = ((2, 1), (1, 1), (3, 1), (2, 0), (1, 0), (3, 0), (0, 1))
ALONG_X = (2, 1, 3)
ALONG_Z = (4, 3, 5, 2, 6, 1, 7)
BF16 = jnp.bfloat16
F32 = jnp.float32
ORDER = (
    ("gate_up", 0, 0), ("gate_up", 0, 1), ("scatter1", 0, 0), ("scatter0", 0, 0),
    ("gate_up", 0, 2), ("up0", 0, 0), ("scatter1", 0, 1), ("scatter0", 0, 1),
    ("up1", 0, 0), ("gate0", 0, 0), ("gate1", 0, 0), ("scatter0", 0, 2),
    ("up0", 0, 1), ("scatter1", 0, 2), ("up1", 0, 1), ("gate_up", 0, 3),
    ("activate", 0, 0), ("gate1", 0, 1), ("gate0", 0, 1), ("gate1", 0, 2),
    ("up1", 0, 2), ("scatter1", 0, 3), ("up0", 0, 2), ("scatter0", 0, 3),
    ("gate0", 0, 2), ("activate", 0, 1), ("forward", 0, 0), ("down", 0, 0),
    ("up1", 0, 3), ("activate", 0, 2), ("gate1", 0, 3), ("up0", 0, 3),
    ("gate0", 0, 3), ("forward", 0, 1), ("down", 0, 1), ("reduce_z", 0, 0),
    ("forward", 0, 2), ("activate", 0, 3), ("down", 0, 2), ("gather_z", 0, 0),
    ("forward", 0, 3), ("reduce_z", 0, 1), ("down", 0, 3), ("reduce_z", 0, 2),
    ("gather_z", 0, 1), ("gate_up", 1, 0), ("gather_z", 0, 2), ("scatter1", 1, 0),
    ("scatter0", 1, 0), ("reduce_z", 0, 3), ("up0", 1, 0), ("gate_up", 1, 1),
    ("up1", 1, 0), ("gate0", 1, 0), ("scatter1", 1, 1), ("gather_z", 0, 3),
    ("gate1", 1, 0), ("scatter0", 1, 1), ("gate_up", 1, 2), ("activate", 1, 0),
    ("scatter1", 1, 2), ("gate0", 1, 1), ("scatter0", 1, 2), ("up1", 1, 1),
    ("gate_up", 1, 3), ("up0", 1, 1), ("up0", 1, 2), ("gate1", 1, 1),
    ("scatter0", 1, 3), ("scatter1", 1, 3), ("gate0", 1, 2), ("up1", 1, 2),
    ("activate", 1, 1), ("up0", 1, 3), ("up1", 1, 3), ("gate1", 1, 2),
    ("gate0", 1, 3), ("forward", 1, 0), ("activate", 1, 2), ("gate1", 1, 3),
    ("down", 1, 0), ("activate", 1, 3), ("forward", 1, 1), ("down", 1, 1),
    ("forward", 1, 2), ("down", 1, 2), ("forward", 1, 3), ("reduce_z", 1, 0),
    ("down", 1, 3), ("reduce_z", 1, 1), ("gather_z", 1, 0), ("reduce_z", 1, 2),
    ("reduce_z", 1, 3), ("gather_z", 1, 1), ("gather_z", 1, 2), ("gather_z", 1, 3),
)


def wait_bytes(ref, sem):
    pltpu.make_async_copy(ref, ref, sem).wait()


def kernel(
    tokens, g0, u0, d0, g1, u1, d1, out,
    wgu, wd, tok, pown, pother, crecv, pother2, crecv2, xsend, xrecv, ysend, yback, msend, mrecv, nsend, nrecv, mown, hid, acc, zsend, zrecv, ysum, yrecv,
    w_s, c_s, r_s, m_s, a_s, f_s, z_s, y_s, t_s, i_s,
):
    gx, gy = lax.axis_index("gx"), lax.axis_index("gy")
    c, chip = lax.rem(gx, 2), gx // 2
    yl, x = lax.rem(chip, 2), chip // 2
    z, yh = lax.rem(gy, 8), gy // 8

    def remote(src, dst, sems, index, device):
        pltpu.make_async_remote_copy(
            src_ref=src, dst_ref=dst, send_sem=sems.at[(0, *index)], recv_sem=sems.at[(1, *index)],
            device_id=device, device_id_type=pl.DeviceIdType.MESH,
        ).start()

    other_core = (chip * 2 + 1 - c, gy)
    other_half = (gx, (1 - yh) * 8 + z)
    other_y = ((x * 2 + 1 - yl) * 2 + c, gy)

    x_at = [lax.rem(x + dx, 4) for dx in range(4)]
    x_device = [((to * 2 + yl) * 2 + c, gy) for to in x_at]
    chip_device = [((x_at[dx] * 2 + lax.rem(yl + dy, 2)) * 2 + c, gy) for dx, dy in OFFSETS]
    z_at = [lax.rem(z + dz, 8) for dz in range(8)]
    z_device = [(gx, yh * 8 + to) for to in z_at]
    partners = [z_device[dz] for dz in ALONG_Z] + [other_half] + chip_device + [other_core]
    barrier = pltpu.get_barrier_semaphore()
    for device in partners:
        pl.semaphore_signal(barrier, inc=1, device_id=device, device_id_type=pl.DeviceIdType.MESH)

    weights = ((g0, u0, d0), (g1, u1, d1))
    halves = [pl.ds(k * HALF, HALF) for k in range(2)]

    def weight_copies(l):
        gate, up, down = weights[l]
        for k in range(2):
            for n, weight in enumerate((gate, up)):
                pltpu.make_async_copy(weight.at[:, halves[k]], wgu.at[l, k, n], w_s.at[l, 0, k, n]).start()
        for k in range(2):
            pltpu.make_async_copy(down.at[halves[k], :], wd.at[l, k], w_s.at[l, 1, k, 0]).start()

    weight_copies(0)
    weight_copies(1)
    for h in range(2):
        tok[0, h, yh, z] = tokens[pl.ds(ROWS * h, ROWS), :]
    pl.semaphore_wait(barrier, len(partners))

    def first_send(h):
        mine = tok.at[0, h, yh, z]
        remote(mine, mine, i_s, (0, h), other_half)

    def first_own(h):
        mine = tok.at[0, h, yh, z]
        for dz in ALONG_Z:
            remote(mine, mine, i_s, (1, h), z_device[dz])

    def first_forward(h):
        theirs = tok.at[0, h, 1 - yh, z]
        wait_bytes(theirs, i_s.at[1, 0, h])
        for dz in ALONG_Z:
            remote(theirs, theirs, i_s, (2, h), z_device[dz])

    core_buffers = ((pother, crecv), (pother2, crecv2))

    def gate_up(l, s):
        h, q = PARTS[s]
        if l == 0:
            if q == 0:
                for n in (1, 2):
                    wait_bytes(tok.at[0, h, 0, pl.ds(0, 7)], i_s.at[1, n, h])
        else:
            wait_bytes(tok.at[1, h, q, pl.ds(0, 7)], t_s.at[1, s])
            for n in range(2):
                wait_bytes(crecv.at[s, n], c_s.at[0, 0, s, n])
        sent, landed = core_buffers[l]
        if s == 0:
            for k in range(2):
                for n in range(2):
                    wait_bytes(wgu.at[l, k, n], w_s.at[l, 0, k, n])
        value = tok[l, h, q].reshape(8 * ROWS, WIDTH)
        for n in (1, 0):
            done = jnp.dot(value, wgu[l, 1 - c, n], preferred_element_type=F32)
            sent[s, n] = done.reshape(4, 2, ROWS, HALF).astype(sent.dtype)
            remote(sent.at[s, n], landed.at[s, n], c_s, (l, s, n), other_core)
        for n in (1, 0):
            done = jnp.dot(value, wgu[l, c, n], preferred_element_type=F32)
            pown[s, n] = done.reshape(4, 2, ROWS, HALF)

    def scatter(l, s, n):
        landed = core_buffers[l][1]
        wait_bytes(landed.at[s, n], c_s.at[1, l, s, n])
        if n == 0:
            for j, side in enumerate((1 - yl, yl)):
                total = pown[s, 0, :, side] + landed[s, 0, :, side].astype(F32)
                xsend[l, s, j] = total.astype(BF16)
                for dx in ALONG_X:
                    remote(xsend.at[l, s, j, x_at[dx]], xrecv.at[l, s, j, dx - 1], r_s, (l, s, j), x_device[dx])
                pown[s, 0, :, side] = total
        else:
            for j in range(2):
                for i in (2 * j, 2 * j + 1):
                    at = x_at[(*ALONG_X, 0)[i]]
                    ysend[l, s, i] = (pown[s, 1, at, 1 - yl] + landed[s, 1, at, 1 - yl].astype(F32)).astype(BF16)
                two = pl.ds(2 * j, 2)
                remote(ysend.at[l, s, two], yback.at[l, s, two], r_s, (l, s, 2 + j), other_y)
            pown[s, 1, :, yl] = pown[s, 1, :, yl] + landed[s, 1, :, yl].astype(F32)

    def middle_gate(l, s, j):
        wait_bytes(xrecv.at[l, s, j], r_s.at[1, l, s, j])
        total = pown[s, 0, x, (1 - yl, yl)[j]]
        for t in range(3):
            total = total + xrecv[l, s, j, t].astype(F32)
        if j == 0:
            msend[l, s] = total.astype(BF16)
            remote(msend.at[l, s], mrecv.at[l, s], m_s, (l, s, 0), other_y)
        else:
            mown[s, 0] = total

    def middle_up(l, s, j):
        two = pl.ds(2 * j, 2)
        wait_bytes(yback.at[l, s, two], r_s.at[1, l, s, 2 + j])
        for i in (2 * j, 2 * j + 1):
            dx = (*ALONG_X, 0)[i]
            total = pown[s, 1, x_at[dx], yl] + yback[l, s, i].astype(F32)
            if dx > 0:
                nsend[l, s, i] = total.astype(BF16)
                remote(nsend.at[l, s, i], nrecv.at[l, s, i], m_s, (l, s, 1), x_device[dx])
            else:
                mown[s, 1] = total

    def activate(l, s):
        wait_bytes(mrecv.at[l, s], m_s.at[1, l, s, 0])
        gate = mown[s, 0] + mrecv[l, s].astype(F32)
        wait_bytes(nrecv.at[l, s], m_s.at[1, l, s, 1])
        up = mown[s, 1]
        for t in range(3):
            up = up + nrecv[l, s, t].astype(F32)
        hid[l, s, c, chip] = (gate / (1.0 + jnp.exp(-gate)) * up).astype(BF16)
        mine = hid.at[l, s, c, chip]
        for device in chip_device:
            remote(mine, mine, a_s, (l, s), device)

    def half_down(l, s, k):
        value = hid[l, s, k].reshape(8 * ROWS, HALF)
        return jnp.dot(value, wd[l, k], preferred_element_type=F32).reshape(8, ROWS, WIDTH)

    def forward(l, s):
        wait_bytes(hid.at[l, s, 0, pl.ds(0, 7)], a_s.at[1, l, s])
        rows = hid.at[l, s, c]
        remote(rows, rows, f_s, (l, s), other_core)
        if s == 0:
            for k in range(2):
                wait_bytes(wd.at[l, k], w_s.at[l, 1, k, 0])
        acc[s] = half_down(l, s, c)

    def down(l, s):
        wait_bytes(hid.at[l, s, 0], f_s.at[1, l, s])
        done = acc[s] + half_down(l, s, 1 - c)
        acc[s] = done
        zsend[l, s] = done.astype(BF16)
        for dz in ALONG_Z:
            remote(zsend.at[l, s, z_at[dz]], zrecv.at[l, s, dz - 1], z_s, (l, s), z_device[dz])

    def reduce_z(l, s):
        wait_bytes(zrecv.at[l, s], z_s.at[1, l, s])
        total = acc[s, z]
        for n in range(7):
            total = total + zrecv[l, s, n].astype(F32)
        ysum[l, s] = total
        remote(ysum.at[l, s], yrecv.at[l, s], y_s, (l, s), other_half)

    def gather_z(l, s):
        h, q = PARTS[s]
        wait_bytes(yrecv.at[l, s], y_s.at[1, l, s])
        total = ysum[l, s] + yrecv[l, s]
        if l == 0:
            tok[1, h, q, z] = total.astype(BF16)
            mine = tok.at[1, h, q, z]
            for dz in ALONG_Z:
                remote(mine, mine, t_s, (s,), z_device[dz])
        else:

            @pl.when(yh == q)
            def _():
                out[pl.ds(ROWS * h, ROWS), :] = total

    steps = {
        "gate_up": gate_up,
        "scatter0": lambda l, s: scatter(l, s, 0),
        "scatter1": lambda l, s: scatter(l, s, 1),
        "gate0": lambda l, s: middle_gate(l, s, 0),
        "gate1": lambda l, s: middle_gate(l, s, 1),
        "up0": lambda l, s: middle_up(l, s, 0),
        "up1": lambda l, s: middle_up(l, s, 1),
        "activate": activate,
        "forward": forward,
        "down": down,
        "reduce_z": reduce_z,
        "gather_z": gather_z,
    }
    first_send(0)
    first_own(0)
    first_send(1)
    first_forward(0)
    first_own(1)
    first_forward(1)
    def drain():
        for h in range(2):
            wait_bytes(tok.at[0, h, 0, 0], i_s.at[0, 0, h])
            for n in (1, 2):
                wait_bytes(tok.at[0, h, 0, pl.ds(0, 7)], i_s.at[0, n, h])
        for s in range(4):
            h, q = PARTS[s]
            wait_bytes(tok.at[1, h, q, pl.ds(0, 7)], t_s.at[0, s])
            for l in range(2):
                for n in range(2):
                    if l == 1:
                        wait_bytes(crecv2.at[s, n], c_s.at[0, l, s, n])
                    wait_bytes(xrecv.at[l, s, n], r_s.at[0, l, s, n])
                    wait_bytes(yback.at[l, s, pl.ds(0, 2)], r_s.at[0, l, s, 2 + n])
                    wait_bytes((mrecv, nrecv)[n].at[l, s], m_s.at[0, l, s, n])
                wait_bytes(hid.at[l, s, 0, pl.ds(0, 7)], a_s.at[0, l, s])
                wait_bytes(hid.at[l, s, 0], f_s.at[0, l, s])
                wait_bytes(zrecv.at[l, s], z_s.at[0, l, s])

    for n, (name, l, s) in enumerate(ORDER):
        if n == len(ORDER) - 1:
            drain()
        steps[name](l, s)
    for l in range(2):
        for s in range(4):
            wait_bytes(yrecv.at[l, s], y_s.at[0, l, s])


def shards(*arrays):
    vmem = pl.BlockSpec(memory_space=pltpu.VMEM)
    anywhere = pl.BlockSpec(memory_space=pl.ANY)
    L, S = 2, len(PARTS)
    sem = pltpu.SemaphoreType.DMA
    return pl.pallas_call(
        kernel,
        out_shape=jax.ShapeDtypeStruct((2 * ROWS, WIDTH), F32),
        in_specs=[vmem] + [anywhere] * 6,
        out_specs=vmem,
        scratch_shapes=[
            pltpu.VMEM((L, 2, 2, WIDTH, HALF), BF16),
            pltpu.VMEM((L, 2, HALF, WIDTH), BF16),
            pltpu.VMEM((L, 2, 2, 8, ROWS, WIDTH), BF16),
            pltpu.VMEM((S, 2, 4, 2, ROWS, HALF), F32),
            pltpu.VMEM((S, 2, 4, 2, ROWS, HALF), F32),
            pltpu.VMEM((S, 2, 4, 2, ROWS, HALF), F32),
            pltpu.VMEM((S, 2, 4, 2, ROWS, HALF), BF16),
            pltpu.VMEM((S, 2, 4, 2, ROWS, HALF), BF16),
            pltpu.VMEM((L, S, 2, 4, ROWS, HALF), BF16),
            pltpu.VMEM((L, S, 2, 3, ROWS, HALF), BF16),
            pltpu.VMEM((L, S, 4, ROWS, HALF), BF16),
            pltpu.VMEM((L, S, 4, ROWS, HALF), BF16),
            pltpu.VMEM((L, S, ROWS, HALF), BF16),
            pltpu.VMEM((L, S, ROWS, HALF), BF16),
            pltpu.VMEM((L, S, 3, ROWS, HALF), BF16),
            pltpu.VMEM((L, S, 3, ROWS, HALF), BF16),
            pltpu.VMEM((S, 2, ROWS, HALF), F32),
            pltpu.VMEM((L, S, 2, 8, ROWS, HALF), BF16),
            pltpu.VMEM((S, 8, ROWS, WIDTH), F32),
            pltpu.VMEM((L, S, 8, ROWS, WIDTH), BF16),
            pltpu.VMEM((L, S, 7, ROWS, WIDTH), BF16),
            pltpu.VMEM((L, S, ROWS, WIDTH), F32),
            pltpu.VMEM((L, S, ROWS, WIDTH), F32),
            sem((L, 2, 2, 2)),
            sem((2, L, S, 2)),
            sem((2, L, S, 4)),
            sem((2, L, S, 2)),
            sem((2, L, S)),
            sem((2, L, S)),
            sem((2, L, S)),
            sem((2, L, S)),
            sem((2, S)),
            sem((2, 3, 2)),
        ],
        compiler_params=pltpu.CompilerParams(collective_id=0, has_side_effects=True, vmem_limit_bytes=56 * 2**20),
        cost_estimate=pl.CostEstimate(flops=6 * 2 * 512 * 512 * 1792, bytes_accessed=6 * 512 * 1792 * 2, transcendentals=0),
    )(*arrays)


def solution(mesh):
    weights = (P("gx", "gy"), P("gx", "gy"), P("gy", "gx"))
    in_specs = (P("gy", "gx"), *weights, *weights)
    return jax.shard_map(shards, mesh=mesh, in_specs=in_specs, out_specs=P("gy", "gx"), check_vma=False)
```

```python
import jax
import jax.numpy as jnp
from jax import lax
from jax.experimental import pallas as pl
from jax.experimental.pallas import tpu as pltpu
from jax.sharding import PartitionSpec as P

PARTS = tuple((h, q) for h in range(2) for q in range(2))
ROWS = 16
WIDTH = 512
HALF = 896
OFFSETS = ((2, 1), (1, 1), (3, 1), (2, 0), (1, 0), (3, 0), (0, 1))
ALONG_X = (2, 1, 3)
ALONG_Z = (4, 3, 5, 2, 6, 1, 7)
BF16 = jnp.bfloat16
F32 = jnp.float32
ORDER = (
    ("gate_up", 0, 1), ("gate_up", 0, 0), ("scatter0", 0, 1), ("scatter1", 0, 1),
    ("scatter0", 0, 0), ("scatter1", 0, 0), ("gate_up", 0, 2), ("up0", 0, 1),
    ("gate_up", 0, 3), ("up1", 0, 1), ("gate1", 0, 1), ("gate0", 0, 1),
    ("scatter1", 0, 2), ("scatter0", 0, 2), ("up0", 0, 0), ("activate", 0, 1),
    ("up1", 0, 2), ("gate1", 0, 2), ("up1", 0, 0), ("up0", 0, 2),
    ("gate0", 0, 0), ("scatter1", 0, 3), ("gate0", 0, 2), ("scatter0", 0, 3),
    ("gate1", 0, 0), ("forward", 0, 1), ("activate", 0, 0), ("down", 0, 1),
    ("up0", 0, 3), ("up1", 0, 3), ("gate1", 0, 3), ("gate0", 0, 3),
    ("activate", 0, 2), ("forward", 0, 0), ("reduce_z", 0, 1), ("down", 0, 0),
    ("activate", 0, 3), ("forward", 0, 2), ("gather_z", 0, 1), ("down", 0, 2),
    ("forward", 0, 3), ("reduce_z", 0, 0), ("down", 0, 3), ("gate_up", 1, 1),
    ("gather_z", 0, 0), ("scatter0", 1, 1), ("reduce_z", 0, 2), ("scatter1", 1, 1),
    ("gather_z", 0, 2), ("gate0", 1, 1), ("reduce_z", 0, 3), ("up0", 1, 1),
    ("gate_up", 1, 0), ("up1", 1, 1), ("scatter1", 1, 0), ("scatter0", 1, 0),
    ("gather_z", 0, 3), ("gate1", 1, 1), ("activate", 1, 1), ("gate_up", 1, 2),
    ("scatter1", 1, 2), ("up0", 1, 0), ("scatter0", 1, 2), ("up1", 1, 0),
    ("gate_up", 1, 3), ("gate0", 1, 0), ("scatter1", 1, 3), ("scatter0", 1, 3),
    ("up0", 1, 2), ("gate1", 1, 2), ("up1", 1, 2), ("forward", 1, 1),
    ("gate1", 1, 0), ("up0", 1, 3), ("gate0", 1, 2), ("gate0", 1, 3),
    ("up1", 1, 3), ("activate", 1, 0), ("down", 1, 1), ("activate", 1, 2),
    ("gate1", 1, 3), ("activate", 1, 3), ("forward", 1, 0), ("down", 1, 0),
    ("forward", 1, 2), ("down", 1, 2), ("forward", 1, 3), ("reduce_z", 1, 1),
    ("down", 1, 3), ("reduce_z", 1, 0), ("gather_z", 1, 1), ("gather_z", 1, 0),
    ("reduce_z", 1, 2), ("reduce_z", 1, 3), ("gather_z", 1, 2), ("gather_z", 1, 3),
)


def wait_bytes(ref, sem):
    pltpu.make_async_copy(ref, ref, sem).wait()


def kernel(
    tokens, g0, u0, d0, g1, u1, d1, out,
    wgu, wd, tok, pown, pother, crecv, pother2, crecv2, xsend, xrecv, ysend, yback, msend, mrecv, nsend, nrecv, mown, hid, acc, zsend, zrecv, ysum, yrecv,
    b_s, w_s, c_s, r_s, m_s, a_s, f_s, z_s, y_s, t_s, i_s,
):
    gx, gy = lax.axis_index("gx"), lax.axis_index("gy")
    c, chip = lax.rem(gx, 2), gx // 2
    yl, x = lax.rem(chip, 2), chip // 2
    z, yh = lax.rem(gy, 8), gy // 8

    def remote(src, dst, sems, index, device):
        pltpu.make_async_remote_copy(
            src_ref=src, dst_ref=dst, send_sem=sems.at[(0, *index)], recv_sem=sems.at[(1, *index)],
            device_id=device, device_id_type=pl.DeviceIdType.MESH,
        ).start()

    other_core = (chip * 2 + 1 - c, gy)
    other_half = (gx, (1 - yh) * 8 + z)
    other_y = ((x * 2 + 1 - yl) * 2 + c, gy)

    x_at = [lax.rem(x + dx, 4) for dx in range(4)]
    x_device = [((to * 2 + yl) * 2 + c, gy) for to in x_at]
    chip_device = [((x_at[dx] * 2 + lax.rem(yl + dy, 2)) * 2 + c, gy) for dx, dy in OFFSETS]
    z_at = [lax.rem(z + dz, 8) for dz in range(8)]
    z_device = [(gx, yh * 8 + to) for to in z_at]
    partners = [z_device[dz] for dz in ALONG_Z] + [other_half] + chip_device + [other_core]
    barrier = pltpu.get_barrier_semaphore()
    for device in partners:
        pl.semaphore_signal(barrier, inc=1, device_id=device, device_id_type=pl.DeviceIdType.MESH)

    met = set()

    def first(*what):
        new = what not in met
        met.add(what)
        return new

    weights = ((g0, u0, d0), (g1, u1, d1))
    halves = [pl.ds(k * HALF, HALF) for k in range(2)]

    def weight_copies(l):
        gate, up, down = weights[l]
        for k in range(2):
            for n, weight in enumerate((gate, up)):
                pltpu.make_async_copy(weight.at[:, halves[k]], wgu.at[l, k, n], w_s.at[l, 0, k, n]).start()
        for k in range(2):
            pltpu.make_async_copy(down.at[halves[k], :], wd.at[l, k], w_s.at[l, 1, k, 0]).start()

    for h in range(2):
        pltpu.make_async_copy(tokens.at[pl.ds(ROWS * h, ROWS), :], tok.at[0, h, yh, z], b_s.at[h]).start()
    weight_copies(0)
    weight_copies(1)
    for h in range(2):
        wait_bytes(tok.at[0, h, yh, z], b_s.at[h])
    pl.semaphore_wait(barrier, len(partners))

    def first_send(h):
        mine = tok.at[0, h, yh, z]
        remote(mine, mine, i_s, (0, h), other_half)

    def first_own(h):
        mine = tok.at[0, h, yh, z]
        for dz in ALONG_Z:
            remote(mine, mine, i_s, (1, h), z_device[dz])

    def first_forward(h):
        theirs = tok.at[0, h, 1 - yh, z]
        wait_bytes(theirs, i_s.at[1, 0, h])
        for dz in ALONG_Z:
            remote(theirs, theirs, i_s, (2, h), z_device[dz])

    core_buffers = ((pother, crecv), (pother2, crecv2))

    def gate_up(l, s):
        h, q = PARTS[s]
        if l == 0:
            if first(0, h):
                for n in (1, 2):
                    wait_bytes(tok.at[0, h, 0, pl.ds(0, 7)], i_s.at[1, n, h])
        else:
            wait_bytes(tok.at[1, h, q, pl.ds(0, 7)], t_s.at[1, s])
            for n in range(2):
                wait_bytes(crecv.at[s, n], c_s.at[0, 0, s, n])
        sent, landed = core_buffers[l]
        if first(1, l):
            for k in range(2):
                for n in range(2):
                    wait_bytes(wgu.at[l, k, n], w_s.at[l, 0, k, n])
        value = tok[l, h, q].reshape(8 * ROWS, WIDTH)
        for n in (1, 0):
            done = jnp.dot(value, wgu[l, 1 - c, n], preferred_element_type=F32)
            sent[s, n] = done.reshape(4, 2, ROWS, HALF).astype(sent.dtype)
            remote(sent.at[s, n], landed.at[s, n], c_s, (l, s, n), other_core)
        for n in (1, 0):
            done = jnp.dot(value, wgu[l, c, n], preferred_element_type=F32)
            pown[s, n] = done.reshape(4, 2, ROWS, HALF)

    def scatter(l, s, n):
        landed = core_buffers[l][1]
        wait_bytes(landed.at[s, n], c_s.at[1, l, s, n])
        if n == 0:
            for j, side in enumerate((1 - yl, yl)):
                total = pown[s, 0, :, side] + landed[s, 0, :, side].astype(F32)
                xsend[l, s, j] = total.astype(BF16)
                for dx in ALONG_X:
                    remote(xsend.at[l, s, j, x_at[dx]], xrecv.at[l, s, j, dx - 1], r_s, (l, s, j), x_device[dx])
                pown[s, 0, :, side] = total
        else:
            for j in range(2):
                for i in (2 * j, 2 * j + 1):
                    at = x_at[(*ALONG_X, 0)[i]]
                    ysend[l, s, i] = (pown[s, 1, at, 1 - yl] + landed[s, 1, at, 1 - yl].astype(F32)).astype(BF16)
                two = pl.ds(2 * j, 2)
                remote(ysend.at[l, s, two], yback.at[l, s, two], r_s, (l, s, 2 + j), other_y)
            pown[s, 1, :, yl] = pown[s, 1, :, yl] + landed[s, 1, :, yl].astype(F32)

    def middle_gate(l, s, j):
        wait_bytes(xrecv.at[l, s, j], r_s.at[1, l, s, j])
        total = pown[s, 0, x, (1 - yl, yl)[j]]
        for t in range(3):
            total = total + xrecv[l, s, j, t].astype(F32)
        if j == 0:
            msend[l, s] = total.astype(BF16)
            remote(msend.at[l, s], mrecv.at[l, s], m_s, (l, s, 0), other_y)
        else:
            mown[s, 0] = total

    def middle_up(l, s, j):
        two = pl.ds(2 * j, 2)
        wait_bytes(yback.at[l, s, two], r_s.at[1, l, s, 2 + j])
        for i in (2 * j, 2 * j + 1):
            dx = (*ALONG_X, 0)[i]
            total = pown[s, 1, x_at[dx], yl] + yback[l, s, i].astype(F32)
            if dx > 0:
                nsend[l, s, i] = total.astype(BF16)
                remote(nsend.at[l, s, i], nrecv.at[l, s, i], m_s, (l, s, 1), x_device[dx])
            else:
                mown[s, 1] = total

    def activate(l, s):
        wait_bytes(mrecv.at[l, s], m_s.at[1, l, s, 0])
        gate = mown[s, 0] + mrecv[l, s].astype(F32)
        wait_bytes(nrecv.at[l, s], m_s.at[1, l, s, 1])
        up = mown[s, 1]
        for t in range(3):
            up = up + nrecv[l, s, t].astype(F32)
        hid[l, s, c, chip] = (gate / (1.0 + jnp.exp(-gate)) * up).astype(BF16)
        mine = hid.at[l, s, c, chip]
        for device in chip_device:
            remote(mine, mine, a_s, (l, s), device)

    def half_down(l, s, k):
        value = hid[l, s, k].reshape(8 * ROWS, HALF)
        return jnp.dot(value, wd[l, k], preferred_element_type=F32).reshape(8, ROWS, WIDTH)

    def forward(l, s):
        wait_bytes(hid.at[l, s, 0, pl.ds(0, 7)], a_s.at[1, l, s])
        rows = hid.at[l, s, c]
        remote(rows, rows, f_s, (l, s), other_core)
        if first(2, l):
            for k in range(2):
                wait_bytes(wd.at[l, k], w_s.at[l, 1, k, 0])
        acc[s] = half_down(l, s, c)

    def down(l, s):
        wait_bytes(hid.at[l, s, 0], f_s.at[1, l, s])
        done = acc[s] + half_down(l, s, 1 - c)
        acc[s] = done
        zsend[l, s] = done.astype(BF16)
        for dz in ALONG_Z:
            remote(zsend.at[l, s, z_at[dz]], zrecv.at[l, s, dz - 1], z_s, (l, s), z_device[dz])

    def reduce_z(l, s):
        wait_bytes(zrecv.at[l, s], z_s.at[1, l, s])
        total = acc[s, z]
        for n in range(7):
            total = total + zrecv[l, s, n].astype(F32)
        ysum[l, s] = total
        remote(ysum.at[l, s], yrecv.at[l, s], y_s, (l, s), other_half)

    def gather_z(l, s):
        h, q = PARTS[s]
        wait_bytes(yrecv.at[l, s], y_s.at[1, l, s])
        total = ysum[l, s] + yrecv[l, s]
        if l == 0:
            tok[1, h, q, z] = total.astype(BF16)
            mine = tok.at[1, h, q, z]
            for dz in ALONG_Z:
                remote(mine, mine, t_s, (s,), z_device[dz])
        else:

            @pl.when(yh == q)
            def _():
                out[pl.ds(ROWS * h, ROWS), :] = total

    steps = {
        "gate_up": gate_up,
        "scatter0": lambda l, s: scatter(l, s, 0),
        "scatter1": lambda l, s: scatter(l, s, 1),
        "gate0": lambda l, s: middle_gate(l, s, 0),
        "gate1": lambda l, s: middle_gate(l, s, 1),
        "up0": lambda l, s: middle_up(l, s, 0),
        "up1": lambda l, s: middle_up(l, s, 1),
        "activate": activate,
        "forward": forward,
        "down": down,
        "reduce_z": reduce_z,
        "gather_z": gather_z,
    }
    first_send(0)
    first_own(0)
    first_send(1)
    first_forward(0)
    first_own(1)
    first_forward(1)
    def drain():
        for h in range(2):
            wait_bytes(tok.at[0, h, 0, 0], i_s.at[0, 0, h])
            for n in (1, 2):
                wait_bytes(tok.at[0, h, 0, pl.ds(0, 7)], i_s.at[0, n, h])
        for s in range(4):
            h, q = PARTS[s]
            wait_bytes(tok.at[1, h, q, pl.ds(0, 7)], t_s.at[0, s])
            for l in range(2):
                for n in range(2):
                    if l == 1:
                        wait_bytes(crecv2.at[s, n], c_s.at[0, l, s, n])
                    wait_bytes(xrecv.at[l, s, n], r_s.at[0, l, s, n])
                    wait_bytes(yback.at[l, s, pl.ds(0, 2)], r_s.at[0, l, s, 2 + n])
                    wait_bytes((mrecv, nrecv)[n].at[l, s], m_s.at[0, l, s, n])
                wait_bytes(hid.at[l, s, 0, pl.ds(0, 7)], a_s.at[0, l, s])
                wait_bytes(hid.at[l, s, 0], f_s.at[0, l, s])
                wait_bytes(zrecv.at[l, s], z_s.at[0, l, s])

    for n, (name, l, s) in enumerate(ORDER):
        if n == len(ORDER) - 1:
            drain()
        steps[name](l, s)
    for l in range(2):
        for s in range(4):
            wait_bytes(yrecv.at[l, s], y_s.at[0, l, s])


def shards(*arrays):
    vmem = pl.BlockSpec(memory_space=pltpu.VMEM)
    anywhere = pl.BlockSpec(memory_space=pl.ANY)
    L, S = 2, len(PARTS)
    sem = pltpu.SemaphoreType.DMA
    return pl.pallas_call(
        kernel,
        out_shape=jax.ShapeDtypeStruct((2 * ROWS, WIDTH), F32),
        in_specs=[anywhere] * 7,
        out_specs=vmem,
        scratch_shapes=[
            pltpu.VMEM((L, 2, 2, WIDTH, HALF), BF16),
            pltpu.VMEM((L, 2, HALF, WIDTH), BF16),
            pltpu.VMEM((L, 2, 2, 8, ROWS, WIDTH), BF16),
            pltpu.VMEM((S, 2, 4, 2, ROWS, HALF), F32),
            pltpu.VMEM((S, 2, 4, 2, ROWS, HALF), F32),
            pltpu.VMEM((S, 2, 4, 2, ROWS, HALF), F32),
            pltpu.VMEM((S, 2, 4, 2, ROWS, HALF), BF16),
            pltpu.VMEM((S, 2, 4, 2, ROWS, HALF), BF16),
            pltpu.VMEM((L, S, 2, 4, ROWS, HALF), BF16),
            pltpu.VMEM((L, S, 2, 3, ROWS, HALF), BF16),
            pltpu.VMEM((L, S, 4, ROWS, HALF), BF16),
            pltpu.VMEM((L, S, 4, ROWS, HALF), BF16),
            pltpu.VMEM((L, S, ROWS, HALF), BF16),
            pltpu.VMEM((L, S, ROWS, HALF), BF16),
            pltpu.VMEM((L, S, 3, ROWS, HALF), BF16),
            pltpu.VMEM((L, S, 3, ROWS, HALF), BF16),
            pltpu.VMEM((S, 2, ROWS, HALF), F32),
            pltpu.VMEM((L, S, 2, 8, ROWS, HALF), BF16),
            pltpu.VMEM((S, 8, ROWS, WIDTH), F32),
            pltpu.VMEM((L, S, 8, ROWS, WIDTH), BF16),
            pltpu.VMEM((L, S, 7, ROWS, WIDTH), BF16),
            pltpu.VMEM((L, S, ROWS, WIDTH), F32),
            pltpu.VMEM((L, S, ROWS, WIDTH), F32),
            sem((2,)),
            sem((L, 2, 2, 2)),
            sem((2, L, S, 2)),
            sem((2, L, S, 4)),
            sem((2, L, S, 2)),
            sem((2, L, S)),
            sem((2, L, S)),
            sem((2, L, S)),
            sem((2, L, S)),
            sem((2, S)),
            sem((2, 3, 2)),
        ],
        compiler_params=pltpu.CompilerParams(collective_id=0, has_side_effects=True, vmem_limit_bytes=56 * 2**20),
        cost_estimate=pl.CostEstimate(flops=6 * 2 * 512 * 512 * 1792, bytes_accessed=6 * 512 * 1792 * 2, transcendentals=0),
    )(*arrays)


def solution(mesh):
    weights = (P("gx", "gy"), P("gx", "gy"), P("gy", "gx"))
    in_specs = (P("gy", "gx"), *weights, *weights)
    return jax.shard_map(shards, mesh=mesh, in_specs=in_specs, out_specs=P("gy", "gx"), check_vma=False)
```

```python
import jax
import jax.numpy as jnp
from jax import lax
from jax.experimental import pallas as pl
from jax.experimental.pallas import tpu as pltpu
from jax.sharding import PartitionSpec as P

PARTS = tuple((h, q) for h in range(2) for q in range(2))
ROWS = 16
WIDTH = 512
HALF = 896
OFFSETS = ((2, 1), (1, 1), (3, 1), (2, 0), (1, 0), (3, 0), (0, 1))
ALONG_X = (2, 1, 3)
ALONG_Z = (4, 3, 5, 2, 6, 1, 7)
BF16 = jnp.bfloat16
F32 = jnp.float32
ORDER = (
    ("gate_up", 0, 0), ("gate_up", 0, 1), ("scatter1", 0, 0), ("scatter0", 0, 0),
    ("gate_up", 0, 2), ("up0", 0, 0), ("scatter1", 0, 1), ("scatter0", 0, 1),
    ("up1", 0, 0), ("gate0", 0, 0), ("gate1", 0, 0), ("scatter0", 0, 2),
    ("up0", 0, 1), ("scatter1", 0, 2), ("up1", 0, 1), ("gate_up", 0, 3),
    ("activate", 0, 0), ("gate1", 0, 1), ("gate0", 0, 1), ("gate1", 0, 2),
    ("up1", 0, 2), ("scatter1", 0, 3), ("up0", 0, 2), ("scatter0", 0, 3),
    ("gate0", 0, 2), ("activate", 0, 1), ("forward", 0, 0), ("down", 0, 0),
    ("up1", 0, 3), ("activate", 0, 2), ("gate1", 0, 3), ("up0", 0, 3),
    ("gate0", 0, 3), ("forward", 0, 1), ("down", 0, 1), ("reduce_z", 0, 0),
    ("forward", 0, 2), ("activate", 0, 3), ("down", 0, 2), ("gather_z", 0, 0),
    ("forward", 0, 3), ("reduce_z", 0, 1), ("down", 0, 3), ("reduce_z", 0, 2),
    ("gather_z", 0, 1), ("gate_up", 1, 0), ("gather_z", 0, 2), ("scatter1", 1, 0),
    ("scatter0", 1, 0), ("reduce_z", 0, 3), ("up0", 1, 0), ("gate_up", 1, 1),
    ("up1", 1, 0), ("gate0", 1, 0), ("scatter1", 1, 1), ("gather_z", 0, 3),
    ("gate1", 1, 0), ("scatter0", 1, 1), ("gate_up", 1, 2), ("activate", 1, 0),
    ("scatter1", 1, 2), ("gate0", 1, 1), ("scatter0", 1, 2), ("up1", 1, 1),
    ("gate_up", 1, 3), ("up0", 1, 1), ("up0", 1, 2), ("gate1", 1, 1),
    ("scatter0", 1, 3), ("scatter1", 1, 3), ("gate0", 1, 2), ("up1", 1, 2),
    ("activate", 1, 1), ("up0", 1, 3), ("up1", 1, 3), ("gate1", 1, 2),
    ("gate0", 1, 3), ("forward", 1, 0), ("activate", 1, 2), ("gate1", 1, 3),
    ("down", 1, 0), ("activate", 1, 3), ("forward", 1, 1), ("down", 1, 1),
    ("forward", 1, 2), ("down", 1, 2), ("forward", 1, 3), ("reduce_z", 1, 0),
    ("down", 1, 3), ("reduce_z", 1, 1), ("gather_z", 1, 0), ("reduce_z", 1, 2),
    ("reduce_z", 1, 3), ("gather_z", 1, 1), ("gather_z", 1, 2), ("gather_z", 1, 3),
)


def wait_bytes(ref, sem):
    pltpu.make_async_copy(ref, ref, sem).wait()


def kernel(
    tokens, g0, u0, d0, g1, u1, d1, out,
    wgu, wd, tok, pown, pother, crecv, pother2, crecv2, xsend, xrecv, ysend, yback, msend, mrecv, nsend, nrecv, mown, hid, acc, zsend, zrecv, ysum, yrecv,
    b_s, w_s, c_s, r_s, m_s, a_s, f_s, z_s, y_s, t_s, i_s,
):
    gx, gy = lax.axis_index("gx"), lax.axis_index("gy")
    c, chip = lax.rem(gx, 2), gx // 2
    yl, x = lax.rem(chip, 2), chip // 2
    z, yh = lax.rem(gy, 8), gy // 8

    def remote(src, dst, sems, index, device):
        pltpu.make_async_remote_copy(
            src_ref=src, dst_ref=dst, send_sem=sems.at[(0, *index)], recv_sem=sems.at[(1, *index)],
            device_id=device, device_id_type=pl.DeviceIdType.MESH,
        ).start()

    other_core = (chip * 2 + 1 - c, gy)
    other_half = (gx, (1 - yh) * 8 + z)
    other_y = ((x * 2 + 1 - yl) * 2 + c, gy)

    x_at = [lax.rem(x + dx, 4) for dx in range(4)]
    x_device = [((to * 2 + yl) * 2 + c, gy) for to in x_at]
    chip_device = [((x_at[dx] * 2 + lax.rem(yl + dy, 2)) * 2 + c, gy) for dx, dy in OFFSETS]
    z_at = [lax.rem(z + dz, 8) for dz in range(8)]
    z_device = [(gx, yh * 8 + to) for to in z_at]
    across = [(gx, (1 - yh) * 8 + z_at[dz]) for dz in (*ALONG_Z, 0)]
    partners = across + [z_device[dz] for dz in ALONG_Z] + chip_device + [other_core]
    barrier = pltpu.get_barrier_semaphore()
    for device in partners:
        pl.semaphore_signal(barrier, inc=1, device_id=device, device_id_type=pl.DeviceIdType.MESH)

    met = set()

    def first(*what):
        new = what not in met
        met.add(what)
        return new

    weights = ((g0, u0, d0), (g1, u1, d1))
    halves = [pl.ds(k * HALF, HALF) for k in range(2)]

    def weight_copies(l):
        gate, up, down = weights[l]
        for k in range(2):
            for n, weight in enumerate((gate, up)):
                pltpu.make_async_copy(weight.at[:, halves[k]], wgu.at[l, k, n], w_s.at[l, 0, k, n]).start()
        for k in range(2):
            pltpu.make_async_copy(down.at[halves[k], :], wd.at[l, k], w_s.at[l, 1, k, 0]).start()

    for h in range(2):
        pltpu.make_async_copy(tokens.at[pl.ds(ROWS * h, ROWS), :], tok.at[0, h, yh, z], b_s.at[h]).start()
    weight_copies(0)
    weight_copies(1)
    for h in range(2):
        wait_bytes(tok.at[0, h, yh, z], b_s.at[h])
    pl.semaphore_wait(barrier, len(partners))

    def first_send(h):
        mine = tok.at[0, h, yh, z]
        for device in across:
            remote(mine, mine, i_s, (0, h), device)
        for dz in ALONG_Z:
            remote(mine, mine, i_s, (1, h), z_device[dz])

    core_buffers = ((pother, crecv), (pother2, crecv2))

    def gate_up(l, s):
        h, q = PARTS[s]
        if l == 0:
            if first(0, h):
                wait_bytes(tok.at[0, h, 0, pl.ds(0, 7)], i_s.at[1, 1, h])
                wait_bytes(tok.at[0, h, 0], i_s.at[1, 0, h])
        else:
            wait_bytes(tok.at[1, h, q, pl.ds(0, 7)], t_s.at[1, s])
            for n in range(2):
                wait_bytes(crecv.at[s, n], c_s.at[0, 0, s, n])
        sent, landed = core_buffers[l]
        if first(1, l):
            for k in range(2):
                for n in range(2):
                    wait_bytes(wgu.at[l, k, n], w_s.at[l, 0, k, n])
        value = tok[l, h, q].reshape(8 * ROWS, WIDTH)
        for n in (1, 0):
            done = jnp.dot(value, wgu[l, 1 - c, n], preferred_element_type=F32)
            sent[s, n] = done.reshape(4, 2, ROWS, HALF).astype(sent.dtype)
            remote(sent.at[s, n], landed.at[s, n], c_s, (l, s, n), other_core)
        for n in (1, 0):
            done = jnp.dot(value, wgu[l, c, n], preferred_element_type=F32)
            pown[s, n] = done.reshape(4, 2, ROWS, HALF)

    def scatter(l, s, n):
        landed = core_buffers[l][1]
        wait_bytes(landed.at[s, n], c_s.at[1, l, s, n])
        if n == 0:
            for j, side in enumerate((1 - yl, yl)):
                total = pown[s, 0, :, side] + landed[s, 0, :, side].astype(F32)
                xsend[l, s, j] = total.astype(BF16)
                for dx in ALONG_X:
                    remote(xsend.at[l, s, j, x_at[dx]], xrecv.at[l, s, j, dx - 1], r_s, (l, s, j), x_device[dx])
                pown[s, 0, :, side] = total
        else:
            for j in range(2):
                for i in (2 * j, 2 * j + 1):
                    at = x_at[(*ALONG_X, 0)[i]]
                    ysend[l, s, i] = (pown[s, 1, at, 1 - yl] + landed[s, 1, at, 1 - yl].astype(F32)).astype(BF16)
                two = pl.ds(2 * j, 2)
                remote(ysend.at[l, s, two], yback.at[l, s, two], r_s, (l, s, 2 + j), other_y)
            pown[s, 1, :, yl] = pown[s, 1, :, yl] + landed[s, 1, :, yl].astype(F32)

    def middle_gate(l, s, j):
        wait_bytes(xrecv.at[l, s, j], r_s.at[1, l, s, j])
        total = pown[s, 0, x, (1 - yl, yl)[j]]
        for t in range(3):
            total = total + xrecv[l, s, j, t].astype(F32)
        if j == 0:
            msend[l, s] = total.astype(BF16)
            remote(msend.at[l, s], mrecv.at[l, s], m_s, (l, s, 0), other_y)
        else:
            mown[s, 0] = total

    def middle_up(l, s, j):
        two = pl.ds(2 * j, 2)
        wait_bytes(yback.at[l, s, two], r_s.at[1, l, s, 2 + j])
        for i in (2 * j, 2 * j + 1):
            dx = (*ALONG_X, 0)[i]
            total = pown[s, 1, x_at[dx], yl] + yback[l, s, i].astype(F32)
            if dx > 0:
                nsend[l, s, i] = total.astype(BF16)
                remote(nsend.at[l, s, i], nrecv.at[l, s, i], m_s, (l, s, 1), x_device[dx])
            else:
                mown[s, 1] = total

    def activate(l, s):
        wait_bytes(mrecv.at[l, s], m_s.at[1, l, s, 0])
        gate = mown[s, 0] + mrecv[l, s].astype(F32)
        wait_bytes(nrecv.at[l, s], m_s.at[1, l, s, 1])
        up = mown[s, 1]
        for t in range(3):
            up = up + nrecv[l, s, t].astype(F32)
        hid[l, s, c, chip] = (gate / (1.0 + jnp.exp(-gate)) * up).astype(BF16)
        mine = hid.at[l, s, c, chip]
        for device in chip_device:
            remote(mine, mine, a_s, (l, s), device)

    def half_down(l, s, k):
        value = hid[l, s, k].reshape(8 * ROWS, HALF)
        return jnp.dot(value, wd[l, k], preferred_element_type=F32).reshape(8, ROWS, WIDTH)

    def forward(l, s):
        wait_bytes(hid.at[l, s, 0, pl.ds(0, 7)], a_s.at[1, l, s])
        rows = hid.at[l, s, c]
        remote(rows, rows, f_s, (l, s), other_core)
        if first(2, l):
            for k in range(2):
                wait_bytes(wd.at[l, k], w_s.at[l, 1, k, 0])
        acc[s] = half_down(l, s, c)

    def down(l, s):
        wait_bytes(hid.at[l, s, 0], f_s.at[1, l, s])
        done = acc[s] + half_down(l, s, 1 - c)
        acc[s] = done
        zsend[l, s] = done.astype(BF16)
        for dz in ALONG_Z:
            remote(zsend.at[l, s, z_at[dz]], zrecv.at[l, s, dz - 1], z_s, (l, s), z_device[dz])

    def reduce_z(l, s):
        wait_bytes(zrecv.at[l, s], z_s.at[1, l, s])
        total = acc[s, z]
        for n in range(7):
            total = total + zrecv[l, s, n].astype(F32)
        ysum[l, s] = total
        remote(ysum.at[l, s], yrecv.at[l, s], y_s, (l, s), other_half)

    def gather_z(l, s):
        h, q = PARTS[s]
        wait_bytes(yrecv.at[l, s], y_s.at[1, l, s])
        total = ysum[l, s] + yrecv[l, s]
        if l == 0:
            tok[1, h, q, z] = total.astype(BF16)
            mine = tok.at[1, h, q, z]
            for dz in ALONG_Z:
                remote(mine, mine, t_s, (s,), z_device[dz])
        else:

            @pl.when(yh == q)
            def _():
                out[pl.ds(ROWS * h, ROWS), :] = total

    steps = {
        "gate_up": gate_up,
        "scatter0": lambda l, s: scatter(l, s, 0),
        "scatter1": lambda l, s: scatter(l, s, 1),
        "gate0": lambda l, s: middle_gate(l, s, 0),
        "gate1": lambda l, s: middle_gate(l, s, 1),
        "up0": lambda l, s: middle_up(l, s, 0),
        "up1": lambda l, s: middle_up(l, s, 1),
        "activate": activate,
        "forward": forward,
        "down": down,
        "reduce_z": reduce_z,
        "gather_z": gather_z,
    }
    first_send(0)
    first_send(1)
    def drain():
        for h in range(2):
            wait_bytes(tok.at[0, h, 0], i_s.at[0, 0, h])
            wait_bytes(tok.at[0, h, 0, pl.ds(0, 7)], i_s.at[0, 1, h])
        for s in range(4):
            h, q = PARTS[s]
            wait_bytes(tok.at[1, h, q, pl.ds(0, 7)], t_s.at[0, s])
            for l in range(2):
                for n in range(2):
                    if l == 1:
                        wait_bytes(crecv2.at[s, n], c_s.at[0, l, s, n])
                    wait_bytes(xrecv.at[l, s, n], r_s.at[0, l, s, n])
                    wait_bytes(yback.at[l, s, pl.ds(0, 2)], r_s.at[0, l, s, 2 + n])
                    wait_bytes((mrecv, nrecv)[n].at[l, s], m_s.at[0, l, s, n])
                wait_bytes(hid.at[l, s, 0, pl.ds(0, 7)], a_s.at[0, l, s])
                wait_bytes(hid.at[l, s, 0], f_s.at[0, l, s])
                wait_bytes(zrecv.at[l, s], z_s.at[0, l, s])

    for n, (name, l, s) in enumerate(ORDER):
        if n == len(ORDER) - 1:
            drain()
        steps[name](l, s)
    for l in range(2):
        for s in range(4):
            wait_bytes(yrecv.at[l, s], y_s.at[0, l, s])


def shards(*arrays):
    vmem = pl.BlockSpec(memory_space=pltpu.VMEM)
    anywhere = pl.BlockSpec(memory_space=pl.ANY)
    L, S = 2, len(PARTS)
    sem = pltpu.SemaphoreType.DMA
    return pl.pallas_call(
        kernel,
        out_shape=jax.ShapeDtypeStruct((2 * ROWS, WIDTH), F32),
        in_specs=[anywhere] * 7,
        out_specs=vmem,
        scratch_shapes=[
            pltpu.VMEM((L, 2, 2, WIDTH, HALF), BF16),
            pltpu.VMEM((L, 2, HALF, WIDTH), BF16),
            pltpu.VMEM((L, 2, 2, 8, ROWS, WIDTH), BF16),
            pltpu.VMEM((S, 2, 4, 2, ROWS, HALF), F32),
            pltpu.VMEM((S, 2, 4, 2, ROWS, HALF), F32),
            pltpu.VMEM((S, 2, 4, 2, ROWS, HALF), F32),
            pltpu.VMEM((S, 2, 4, 2, ROWS, HALF), BF16),
            pltpu.VMEM((S, 2, 4, 2, ROWS, HALF), BF16),
            pltpu.VMEM((L, S, 2, 4, ROWS, HALF), BF16),
            pltpu.VMEM((L, S, 2, 3, ROWS, HALF), BF16),
            pltpu.VMEM((L, S, 4, ROWS, HALF), BF16),
            pltpu.VMEM((L, S, 4, ROWS, HALF), BF16),
            pltpu.VMEM((L, S, ROWS, HALF), BF16),
            pltpu.VMEM((L, S, ROWS, HALF), BF16),
            pltpu.VMEM((L, S, 3, ROWS, HALF), BF16),
            pltpu.VMEM((L, S, 3, ROWS, HALF), BF16),
            pltpu.VMEM((S, 2, ROWS, HALF), F32),
            pltpu.VMEM((L, S, 2, 8, ROWS, HALF), BF16),
            pltpu.VMEM((S, 8, ROWS, WIDTH), F32),
            pltpu.VMEM((L, S, 8, ROWS, WIDTH), BF16),
            pltpu.VMEM((L, S, 7, ROWS, WIDTH), BF16),
            pltpu.VMEM((L, S, ROWS, WIDTH), F32),
            pltpu.VMEM((L, S, ROWS, WIDTH), F32),
            sem((2,)),
            sem((L, 2, 2, 2)),
            sem((2, L, S, 2)),
            sem((2, L, S, 4)),
            sem((2, L, S, 2)),
            sem((2, L, S)),
            sem((2, L, S)),
            sem((2, L, S)),
            sem((2, L, S)),
            sem((2, S)),
            sem((2, 2, 2)),
        ],
        compiler_params=pltpu.CompilerParams(collective_id=0, has_side_effects=True, vmem_limit_bytes=56 * 2**20),
        cost_estimate=pl.CostEstimate(flops=6 * 2 * 512 * 512 * 1792, bytes_accessed=6 * 512 * 1792 * 2, transcendentals=0),
    )(*arrays)


def solution(mesh):
    weights = (P("gx", "gy"), P("gx", "gy"), P("gy", "gx"))
    in_specs = (P("gy", "gx"), *weights, *weights)
    return jax.shard_map(shards, mesh=mesh, in_specs=in_specs, out_specs=P("gy", "gx"), check_vma=False)
```
